32 devices in a mesh: row: 4 (over x, core), col: 8 (over z, y).
Axes of the slice: x: 2, y: 2, z: 4, core: 2. Of those that a mesh axis runs over, the one named last changes fastest.
Arguments:
- ham: bfloat16 [3072, 3072], P('row', 'col'), may hold values from -0.109375 to 0.109375
- deriv: bfloat16 [3072, 3072], P('row', 'col'), may hold values from -6 to 6
- band: int32 [24], replicated, may hold values from 1 to 12, as said below
- frag_of: int32 [24], replicated, may hold values from 0 to 15
Outputs:
- sign_iterate: bfloat16 [3072, 3072], P('row', 'col')
- energy_density: bfloat16 [3072, 3072], P('row', 'col')
- pulay_terms: float32 [16, 128], P('col')
The draws below stay inside these ranges and needn't reach their ends.
Inputs may be any that keep to these rules, and one draw needn't show every extreme that they name: Some block row has band half-width exactly 12.
All inputs are finite; a program needn't handle non-finite values.
Results may differ from the reference program's by a relative error of at most 0.006.
Values may be sent and summed in bfloat16 or wider, within the bound.
No kernel may reach another device: no remote copies, remote signals or barrier semaphores. Data moves between devices by JAX's collectives and lax.ppermute only.
A program may use at most 64 MiB of HBM per device.

```python
import jax
import jax.numpy as jnp
from jax import lax

BLK = 128
WMIN = 1
NB = 24
WMAX = 12
ORDER = 3072
FRAGS = 16


def draw_band(key, part):
    first_key = jax.random.fold_in(key, 11)
    second_key = jax.random.fold_in(key, 23)
    widths = jax.random.randint(first_key, (NB,), WMIN, WMAX + 1, dtype=jnp.int32)
    chosen = jax.random.randint(second_key, (), 0, NB, dtype=jnp.int32)
    places = jnp.arange(NB, dtype=jnp.int32)
    return jnp.where(places == chosen, jnp.int32(WMAX), widths).astype(jnp.int32)


def place_ends(values, own_key, low, high):
    place = [jax.random.randint(jax.random.fold_in(own_key, axis), (), 0, length) for axis, length in enumerate(values.shape)]
    longest = values.shape.index(max(values.shape))
    neighbour = place[:longest] + [(place[longest] + 1) % values.shape[longest]] + place[longest + 1:]
    return values.at[tuple(place)].set(low).at[tuple(neighbour)].set(high)


def block_levels(rng, extent, cuts, least, top_value):
    gain = 1.0
    for position, shards_of in cuts:
        draws = jax.random.uniform(jax.random.fold_in(jax.random.fold_in(rng, 6), position), (shards_of,), jnp.float32, least / len(cuts), top_value / len(cuts))
        gain = gain * jnp.repeat(jnp.exp(draws), extent[position] // shards_of).reshape((-1,) + (1,) * (len(extent) - 1 - position))
    return gain


def gaussian(key, extent, width, limit, shards=(), kind=jnp.bfloat16):
    result = jax.random.normal(key, extent, jnp.float32) * width
    if len(shards) > 0:
        result = block_levels(key, extent, shards, -0.22, 0.18) * result
    return jnp.clip(result, min=-limit, max=limit).astype(kind)


def setup_inputs(seed: int = 0) -> dict:
    streams_of = jax.random.split(jax.random.key(seed), 5)
    ham = gaussian(streams_of[0], (ORDER, ORDER), (BLK * (2 * WMAX + 1)) ** -0.5, 0.109375, ((0, 4), (1, 8)))
    deriv = gaussian(streams_of[1], (ORDER, ORDER), 1.0, 6.0, ((0, 4), (1, 8)))
    band = draw_band(jax.random.fold_in(streams_of[4], 71), 0)
    frag_of = place_ends(jax.random.randint(streams_of[3], (NB,), 0, FRAGS), jax.random.fold_in(streams_of[3], 1), 0, FRAGS - 1).astype(jnp.int32)
    return dict(ham=ham, deriv=deriv, band=band, frag_of=frag_of)


def pattern_of(band):
    blocks = jnp.arange(NB, dtype=jnp.int32)
    widest = jnp.maximum(band[:, None], band[None, :])
    inside = jnp.abs(blocks[:, None] - blocks[None, :]) <= widest
    block_mask = inside.astype(jnp.float32)
    return jnp.repeat(jnp.repeat(block_mask, BLK, axis=0), BLK, axis=1)


def reference(ham, deriv, band, frag_of):
    pattern = pattern_of(band)
    start = (ham.astype(jnp.float32) * pattern).astype(jnp.bfloat16)
    square = (jnp.dot(start, start, preferred_element_type=jnp.float32) * pattern).astype(jnp.bfloat16)
    cubic = jnp.dot(start, square, preferred_element_type=jnp.float32)
    sign_iterate = (pattern * (1.5 * start.astype(jnp.float32) - 0.5 * cubic)).astype(jnp.bfloat16)
    identity = jnp.eye(ORDER, dtype=jnp.float32)
    density = (0.5 * (identity - sign_iterate.astype(jnp.float32))).astype(jnp.bfloat16)
    weighted = (jnp.dot(start, density, preferred_element_type=jnp.float32) * pattern).astype(jnp.bfloat16)
    energy_density = (jnp.dot(density, weighted, preferred_element_type=jnp.float32) * pattern).astype(jnp.bfloat16)
    column_terms = jnp.sum(energy_density.astype(jnp.float32) * deriv.astype(jnp.float32), axis=0).reshape(NB, BLK)
    fragments = jnp.arange(FRAGS, dtype=jnp.int32)
    onehot = (frag_of[None, :] == fragments[:, None]).astype(jnp.float32)
    pulay_terms = jnp.dot(onehot, column_terms, precision=lax.Precision.HIGHEST)
    return sign_iterate, energy_density, pulay_terms
```

```python
import functools

import jax
import jax.numpy as jnp
from jax import lax
from jax.experimental import pallas as pl
from jax.experimental.pallas import tpu as pltpu
from jax.sharding import PartitionSpec as P

BLK = 128
FRAG_DEV = 2
AXES = ("row", "col")
VMEM_LIMIT = 48 * 1024 * 1024


def cycle_of(count):
    width = 1
    while (2 * width) ** 2 <= count:
        width *= 2
    depth = count // width
    walk = [(step, 0) for step in range(depth)]
    for turn, step in enumerate(range(depth - 1, -1, -1)):
        across = list(range(1, width))
        walk += [(step, place) for place in (across[::-1] if turn % 2 else across)]
    return [step * width + place for step, place in walk]


class Plan:
    def __init__(self, rows_here, cols_here):
        self.rows = lax.axis_size("row")
        self.cols = lax.axis_size("col")
        self.rows_here = rows_here
        self.cols_here = cols_here
        self.parts = rows_here // cols_here
        self.block_rows = rows_here // BLK
        self.block_cols = cols_here // BLK
        self.widest = self.rows * self.block_rows // 2
        self.cycle = cycle_of(self.cols)
        self.schedule = []
        half = self.cols // 2
        for distance in range(1, half + 1):
            for part in range(self.parts):
                for direction in (1, -1):
                    if distance < half or direction == (1 if part % 2 == 0 else -1):
                        self.schedule.append((part, distance, direction))

    def piece_is_zero(self, row, part, col):
        first_row = row * self.block_rows + part * self.block_cols
        first_col = col * self.block_cols
        gap = abs(first_row - first_col) - (self.block_cols - 1)
        return gap > self.widest

    def ring_pairs(self, part, distance, direction):
        pairs = []
        for row in range(self.rows):
            for place in range(self.cols):
                origin = self.cycle[(place - direction * (distance - 1)) % self.cols]
                if self.piece_is_zero(row, part, origin):
                    continue
                source = self.cycle[place]
                target = self.cycle[(place + direction) % self.cols]
                pairs.append((row * self.cols + source, row * self.cols + target))
        return pairs

    def left_order(self):
        return [(part, 0, 1) for part in range(self.parts)] + self.schedule

    def origin_col(self, distance, direction):
        col = lax.axis_index("col")
        result = col
        if distance:
            result = jnp.int32(0)
            for place in range(self.cols):
                origin = self.cycle[(place - direction * distance) % self.cols]
                result = jnp.where(col == self.cycle[place], jnp.int32(origin), result)
        return result


def ring_gather(plan, pieces):
    held = {(part, direction): pieces[part] for part in range(plan.parts) for direction in (1, -1)}
    received = []
    for part, distance, direction in plan.schedule:
        value = lax.ppermute(held[part, direction], AXES, plan.ring_pairs(part, distance, direction))
        held[part, direction] = value
        received.append(value)
    return list(pieces) + received


def row_exchange(plan, pieces):
    found = {}
    for part, piece in enumerate(pieces):
        found[0, part] = piece
        for other in range(2, plan.rows, 2):
            found[other, part] = lax.ppermute(piece, "row", [(i, i ^ other) for i in range(plan.rows)])
    for part in range(plan.parts):
        for other in range(0, plan.rows, 2):
            found[other + 1, part] = lax.ppermute(found[other, part], "row", [(i, i ^ 1) for i in range(plan.rows)])
    return [found[other, part] for other in range(plan.rows) for part in range(plan.parts)]


def block_inside(plan, band_ref, block_row, block_col):
    row = lax.axis_index("row") * plan.block_rows + block_row
    col = lax.axis_index("col") * plan.block_cols + block_col
    return jnp.abs(row - col) <= jnp.maximum(band_ref[row], band_ref[col])


def masked(plan, band_ref, value, part, fill=0.0):
    lines = []
    for i in range(plan.block_cols):
        line = []
        for j in range(plan.block_cols):
            keep = block_inside(plan, band_ref, part * plan.block_cols + i, j)
            block = value[i * BLK : (i + 1) * BLK, j * BLK : (j + 1) * BLK]
            line.append(block * keep.astype(jnp.float32))
        lines.append(jnp.concatenate(line, axis=1))
    return jnp.concatenate(lines, axis=0)


def kernel_call(plan, kernel, outs, band, arrays, flops):
    vmem = pl.BlockSpec(memory_space=pltpu.VMEM)
    smem = pl.BlockSpec(memory_space=pltpu.SMEM)
    moved = sum(a.size * a.dtype.itemsize for a in arrays) + sum(o.size * o.dtype.itemsize for o in outs)
    scratch = [pltpu.VMEM((plan.rows * plan.rows_here, plan.cols_here), jnp.bfloat16)]
    return pl.pallas_call(
        kernel,
        out_shape=outs,
        in_specs=[smem] + [vmem] * len(arrays),
        out_specs=[vmem] * len(outs),
        scratch_shapes=scratch,
        compiler_params=pltpu.CompilerParams(vmem_limit_bytes=VMEM_LIMIT),
        cost_estimate=pl.CostEstimate(flops=flops, bytes_accessed=moved, transcendentals=0),
    )(band, *arrays)


def piece_shape(plan, dtype=jnp.bfloat16):
    return jax.ShapeDtypeStruct((plan.cols_here, plan.cols_here), dtype)


def mask_kernel(plan, band_ref, ham_ref, *refs):
    for part in range(plan.parts):
        lines = pl.ds(part * plan.cols_here, plan.cols_here)
        value = ham_ref[lines, :].astype(jnp.float32)
        refs[part][...] = masked(plan, band_ref, value, part).astype(jnp.bfloat16)


def product(plan, left_refs, right_refs, right_all, part):
    if part == 0:
        row = lax.axis_index("row")
        for other in range(plan.rows):
            for piece in range(plan.parts):
                first = (row ^ other) * plan.rows_here + piece * plan.cols_here
                lines = pl.ds(pl.multiple_of(first, plan.cols_here), plan.cols_here)
                right_all[lines, :] = right_refs[other * plan.parts + piece][...]
    total = None
    for place, (of_part, distance, direction) in enumerate(plan.left_order()):
        if of_part != part:
            continue
        first = plan.origin_col(distance, direction) * plan.cols_here
        lines = pl.ds(pl.multiple_of(first, plan.cols_here), plan.cols_here)
        term = jnp.dot(left_refs[place][...], right_all[lines, :], preferred_element_type=jnp.float32)
        total = term if total is None else total + term
    return total


def split_refs(plan, refs):
    lefts = plan.parts * plan.cols
    rights = plan.parts * plan.rows
    return refs[:lefts], refs[lefts : lefts + rights], refs[lefts + rights :]


def product_kernel(plan, band_ref, *refs):
    left_refs, right_refs, (*out_refs, right_all) = split_refs(plan, refs)
    for part in range(plan.parts):
        total = product(plan, left_refs, right_refs, right_all, part)
        out_refs[part][...] = masked(plan, band_ref, total, part).astype(jnp.bfloat16)


def sign_kernel(plan, band_ref, *refs):
    left_refs, right_refs, (sign_ref, *out_refs, right_all) = split_refs(plan, refs)
    n = plan.cols_here
    for part in range(plan.parts):
        total = product(plan, left_refs, right_refs, right_all, part)
        start = left_refs[part][...].astype(jnp.float32)
        sign = masked(plan, band_ref, 1.5 * start - 0.5 * total, part).astype(jnp.bfloat16)
        sign_ref[part * n : (part + 1) * n, :] = sign
        first_row = lax.axis_index("row") * plan.rows_here + part * n
        first_col = lax.axis_index("col") * n
        rows = first_row + lax.broadcasted_iota(jnp.int32, (n, n), 0)
        cols = first_col + lax.broadcasted_iota(jnp.int32, (n, n), 1)
        identity = (rows == cols).astype(jnp.float32)
        out_refs[part][...] = (0.5 * (identity - sign.astype(jnp.float32))).astype(jnp.bfloat16)


def energy_kernel(plan, band_ref, frag_ref, deriv_ref, *refs):
    left_refs, right_refs, (energy_ref, sums_ref, right_all) = split_refs(plan, refs)
    n = plan.cols_here
    terms = None
    for part in range(plan.parts):
        total = product(plan, left_refs, right_refs, right_all, part)
        energy = masked(plan, band_ref, total, part).astype(jnp.bfloat16)
        lines = pl.ds(part * n, n)
        energy_ref[lines, :] = energy
        weighed = energy.astype(jnp.float32) * deriv_ref[lines, :].astype(jnp.float32)
        term = jnp.sum(weighed, axis=0, keepdims=True)
        terms = term if terms is None else terms + term
    count = FRAG_DEV * plan.cols
    fragment = lax.broadcasted_iota(jnp.int32, (count, BLK), 0)
    sums = jnp.zeros((count, BLK), jnp.float32)
    for j in range(plan.block_cols):
        owner = frag_ref[lax.axis_index("col") * plan.block_cols + j]
        line = jnp.broadcast_to(terms[:, j * BLK : (j + 1) * BLK], (count, BLK))
        sums = sums + jnp.where(fragment == owner, line, 0.0)
    sums_ref[...] = sums


def body(ham, deriv, band, frag_of):
    plan = Plan(*ham.shape)
    flops = 2 * plan.rows_here * plan.rows * plan.rows_here * plan.cols_here
    pieces = [piece_shape(plan)] * plan.parts
    whole = jax.ShapeDtypeStruct(ham.shape, jnp.bfloat16)
    count = FRAG_DEV * plan.cols

    start = kernel_call(plan, functools.partial(mask_kernel, plan), pieces, band, [ham], 0)
    slab = ring_gather(plan, start)
    column = row_exchange(plan, start)
    square = kernel_call(plan, functools.partial(product_kernel, plan), pieces, band, slab + column, flops)
    column = row_exchange(plan, square)
    sign_iterate, *density = kernel_call(
        plan, functools.partial(sign_kernel, plan), [whole] + pieces, band, slab + column, flops
    )
    column = row_exchange(plan, density)
    density_slab = ring_gather(plan, density)
    weighted = kernel_call(plan, functools.partial(product_kernel, plan), pieces, band, slab + column, flops)
    column = row_exchange(plan, weighted)

    vmem = pl.BlockSpec(memory_space=pltpu.VMEM)
    smem = pl.BlockSpec(memory_space=pltpu.SMEM)
    arrays = [deriv] + density_slab + column
    energy_density, sums = pl.pallas_call(
        functools.partial(energy_kernel, plan),
        out_shape=[whole, jax.ShapeDtypeStruct((count, BLK), jnp.float32)],
        in_specs=[smem, smem] + [vmem] * len(arrays),
        out_specs=[vmem, vmem],
        scratch_shapes=[pltpu.VMEM((plan.rows * plan.rows_here, plan.cols_here), jnp.bfloat16)],
        compiler_params=pltpu.CompilerParams(vmem_limit_bytes=VMEM_LIMIT),
        cost_estimate=pl.CostEstimate(flops=flops, bytes_accessed=8 * ham.size, transcendentals=0),
    )(band, frag_of, *arrays)

    sums = sums.reshape(1, plan.cols, FRAG_DEV, BLK)
    sums = jnp.broadcast_to(sums, (plan.rows, plan.cols, FRAG_DEV, BLK))
    sums = sums.reshape(plan.rows * plan.cols, FRAG_DEV, BLK)
    pulay_terms = jnp.sum(lax.all_to_all(sums, AXES, 0, 0), axis=0)
    return (sign_iterate, energy_density, pulay_terms)


def solution(mesh):
    placed = (P("row", "col"), P("row", "col"), P(), P())
    return jax.shard_map(
        body,
        mesh=mesh,
        in_specs=placed,
        out_specs=(P("row", "col"), P("row", "col"), P("col", None)),
        check_vma=False,
    )
```

```python
import functools

import jax
import jax.numpy as jnp
from jax import lax
from jax.experimental import pallas as pl
from jax.experimental.pallas import tpu as pltpu
from jax.sharding import PartitionSpec as P

BLK = 128
FRAG_DEV = 2
AXES = ("row", "col")
SPARE_VMEM = 10 * 1024 * 1024


def cycle_of(count):
    width = 1
    while (2 * width) ** 2 <= count:
        width *= 2
    depth = count // width
    walk = [(step, 0) for step in range(depth)]
    for turn, step in enumerate(range(depth - 1, -1, -1)):
        across = list(range(1, width))
        walk += [(step, place) for place in (across[::-1] if turn % 2 else across)]
    return [step * width + place for step, place in walk]


class Plan:
    def __init__(self, rows_here, cols_here):
        self.rows = lax.axis_size("row")
        self.cols = lax.axis_size("col")
        self.rows_here = rows_here
        self.cols_here = cols_here
        self.order = self.rows * rows_here
        self.block_rows = rows_here // BLK
        self.block_cols = cols_here // BLK
        self.cycle = cycle_of(self.cols)
        self.far = self.cols // 2

    def ring(self, value):
        pairs = []
        for row in range(self.rows):
            direction = -1 if row % 2 else 1
            for place in range(self.cols):
                target = self.cycle[(place + direction) % self.cols]
                pairs.append((row * self.cols + self.cycle[place], row * self.cols + target))
        return lax.ppermute(value, AXES, pairs)

    def across(self, value, other):
        return lax.ppermute(value, "row", [(i, i ^ other) for i in range(self.rows)])

    def origin_first(self, distance, behind):
        col = lax.axis_index("col")
        forward = (lax.axis_index("row") % 2 == 0) == behind
        origin = jnp.int32(0)
        for place in range(self.cols):
            before = self.cycle[(place - distance) % self.cols]
            after = self.cycle[(place + distance) % self.cols]
            source = jnp.where(forward, jnp.int32(before), jnp.int32(after))
            origin = jnp.where(col == self.cycle[place], source, origin)
        return pl.multiple_of(origin * self.cols_here, self.cols_here)

    def row_first(self, other):
        return pl.multiple_of((lax.axis_index("row") ^ other) * self.rows_here, self.rows_here)


def masked(plan, band_ref, value):
    lines = []
    for i in range(plan.block_rows):
        line = []
        for j in range(plan.block_cols):
            row = lax.axis_index("row") * plan.block_rows + i
            col = lax.axis_index("col") * plan.block_cols + j
            keep = jnp.abs(row - col) <= jnp.maximum(band_ref[row], band_ref[col])
            block = value[i * BLK : (i + 1) * BLK, j * BLK : (j + 1) * BLK]
            line.append(block * keep.astype(jnp.float32))
        lines.append(jnp.concatenate(line, axis=1))
    return jnp.concatenate(lines, axis=0)


def dot(left, right):
    return jnp.dot(left, right, preferred_element_type=jnp.float32)


def call(kernel, outs, scalars, arrays, flops, aliases=None):
    vmem = pl.BlockSpec(memory_space=pltpu.VMEM)
    smem = pl.BlockSpec(memory_space=pltpu.SMEM)
    moved = sum(a.size * a.dtype.itemsize for a in list(arrays) + list(outs))
    return pl.pallas_call(
        kernel,
        out_shape=outs,
        in_specs=[smem] * len(scalars) + [vmem] * len(arrays),
        out_specs=[vmem] * len(outs),
        input_output_aliases=aliases or {},
        compiler_params=pltpu.CompilerParams(vmem_limit_bytes=moved + SPARE_VMEM),
        cost_estimate=pl.CostEstimate(flops=flops, bytes_accessed=moved, transcendentals=0),
    )(*scalars, *arrays)


def mask_kernel(plan, band_ref, ham_ref, out_ref):
    out_ref[...] = masked(plan, band_ref, ham_ref[...].astype(jnp.float32)).astype(jnp.bfloat16)


def near_kernel(plan, keep_slab, *refs):
    rights, refs = refs[: plan.rows], refs[plan.rows :]
    count = 2 * plan.far - 1
    lefts, (total_ref, right_ref, *slab_ref) = refs[:count], refs[count:]
    for other in range(plan.rows):
        right_ref[pl.ds(plan.row_first(other), plan.rows_here), :] = rights[other][...]
    total = None
    for place, left in enumerate(lefts):
        first = plan.origin_first((place + 1) // 2, place % 2 == 1)
        if keep_slab:
            slab_ref[0][:, pl.ds(first, plan.cols_here)] = left[...]
        term = dot(left[...], right_ref[pl.ds(first, plan.cols_here), :])
        total = term if total is None else total + term
    total_ref[...] = total


def far_terms(plan, total_ref, right_ref, far_ref):
    first = plan.origin_first(plan.far, True)
    return total_ref[...] + dot(far_ref[...], right_ref[pl.ds(first, plan.cols_here), :])


def square_kernel(plan, band_ref, total_ref, right_ref, far_ref, _, out_ref, slab_ref):
    total = far_terms(plan, total_ref, right_ref, far_ref)
    slab_ref[:, pl.ds(plan.origin_first(plan.far, True), plan.cols_here)] = far_ref[...]
    out_ref[...] = masked(plan, band_ref, total).astype(jnp.bfloat16)


def slab_terms(plan, slab_ref, pieces):
    total = None
    for other, piece in pieces:
        term = dot(slab_ref[:, pl.ds(plan.row_first(other), plan.rows_here)], piece[...])
        total = term if total is None else total + term
    return total


def some_kernel(plan, others, slab_ref, *refs):
    *pieces, total_ref = refs
    total_ref[...] = slab_terms(plan, slab_ref, list(zip(others, pieces)))


def sign_kernel(plan, others, band_ref, slab_ref, total_ref, start_ref, *refs):
    *pieces, sign_ref, density_ref = refs
    cubic = total_ref[...] + slab_terms(plan, slab_ref, list(zip(others, pieces)))
    sign = masked(plan, band_ref, 1.5 * start_ref[...].astype(jnp.float32) - 0.5 * cubic).astype(jnp.bfloat16)
    sign_ref[...] = sign
    first_row = lax.axis_index("row") * plan.rows_here
    first_col = lax.axis_index("col") * plan.cols_here
    rows = first_row + lax.broadcasted_iota(jnp.int32, sign.shape, 0)
    cols = first_col + lax.broadcasted_iota(jnp.int32, sign.shape, 1)
    identity = (rows == cols).astype(jnp.float32)
    density_ref[...] = (0.5 * (identity - sign.astype(jnp.float32))).astype(jnp.bfloat16)


def weighted_kernel(plan, others, band_ref, slab_ref, *refs):
    *pieces, out_ref = refs
    total = slab_terms(plan, slab_ref, list(zip(others, pieces)))
    out_ref[...] = masked(plan, band_ref, total).astype(jnp.bfloat16)


def energy_kernel(plan, band_ref, frag_ref, total_ref, right_ref, far_ref, deriv_ref, energy_ref, sums_ref):
    total = far_terms(plan, total_ref, right_ref, far_ref)
    energy = masked(plan, band_ref, total).astype(jnp.bfloat16)
    energy_ref[...] = energy
    weighed = energy.astype(jnp.float32) * deriv_ref[...].astype(jnp.float32)
    terms = jnp.sum(weighed, axis=0, keepdims=True)
    count = FRAG_DEV * plan.cols
    fragment = lax.broadcasted_iota(jnp.int32, (count, BLK), 0)
    sums = jnp.zeros((count, BLK), jnp.float32)
    for j in range(plan.block_cols):
        owner = frag_ref[lax.axis_index("col") * plan.block_cols + j]
        line = jnp.broadcast_to(terms[:, j * BLK : (j + 1) * BLK], (count, BLK))
        sums = sums + jnp.where(fragment == owner, line, 0.0)
    sums_ref[...] = sums


def body(ham, deriv, band, frag_of):
    plan = Plan(*ham.shape)
    bind = functools.partial
    flops = 2 * plan.rows_here * plan.order * plan.cols_here
    block = jax.ShapeDtypeStruct(ham.shape, jnp.bfloat16)
    total_type = jax.ShapeDtypeStruct(ham.shape, jnp.float32)
    slab_type = jax.ShapeDtypeStruct((plan.rows_here, plan.order), jnp.bfloat16)
    column_type = jax.ShapeDtypeStruct((plan.order, plan.cols_here), jnp.bfloat16)
    others = range(plan.rows)

    def exchange_start(value):
        return [plan.across(value, other) for other in range(2, plan.rows, 2)]

    def exchange_end(first_two, crossed):
        return list(first_two) + [piece for value in crossed for piece in (value, plan.across(value, 1))]

    def gather(mine, partner):
        shards = [mine]
        for distance in range(1, plan.far):
            mine = plan.ring(mine)
            partner = plan.ring(partner)
            shards += [mine, plan.across(partner, 1)]
        return shards, plan.ring(mine)

    (start,) = call(bind(mask_kernel, plan), [block], [band], [ham], 0)
    partner = plan.across(start, 1)
    shards, far = gather(start, partner)
    column = exchange_end([start, partner], exchange_start(start))
    total, right, slab = call(
        bind(near_kernel, plan, True), [total_type, column_type, slab_type], [], column + shards, flops
    )
    square, slab = call(
        bind(square_kernel, plan), [block, slab_type], [band], [total, right, far, slab], flops // 8, {4: 1}
    )

    crossed = exchange_start(square)
    partner = plan.across(square, 1)
    (total,) = call(bind(some_kernel, plan, [0, 1]), [total_type], [], [slab, square, partner], flops // 2)
    column = exchange_end([square, partner], crossed)
    sign_iterate, density = call(
        bind(sign_kernel, plan, list(others)[2:]), [block, block], [band], [slab, total, start] + column[2:], flops // 2
    )

    partner = plan.across(density, 1)
    shards, far = gather(density, partner)
    column = exchange_end([density, partner], exchange_start(density))
    (weighted,) = call(bind(weighted_kernel, plan, others), [block], [band], [slab] + column, flops)
    column = exchange_end([weighted, plan.across(weighted, 1)], exchange_start(weighted))
    total, right = call(bind(near_kernel, plan, False), [total_type, column_type], [], column + shards, flops)
    energy_density, sums = call(
        bind(energy_kernel, plan),
        [block, jax.ShapeDtypeStruct((FRAG_DEV * plan.cols, BLK), jnp.float32)],
        [band, frag_of],
        [total, right, far, deriv],
        flops // 8,
    )
    sums = sums.reshape(1, plan.cols, FRAG_DEV, BLK)
    sums = jnp.broadcast_to(sums, (plan.rows, plan.cols, FRAG_DEV, BLK))
    sums = sums.reshape(plan.rows * plan.cols, FRAG_DEV, BLK)
    pulay_terms = jnp.sum(lax.all_to_all(sums, AXES, 0, 0), axis=0)
    return (sign_iterate, energy_density, pulay_terms)


def solution(mesh):
    placed = (P("row", "col"), P("row", "col"), P(), P())
    return jax.shard_map(
        body,
        mesh=mesh,
        in_specs=placed,
        out_specs=(P("row", "col"), P("row", "col"), P("col", None)),
        check_vma=False,
    )
```

```python
import functools

import jax
import jax.numpy as jnp
from jax import lax
from jax.experimental import pallas as pl
from jax.experimental.pallas import tpu as pltpu
from jax.sharding import PartitionSpec as P

BLK = 128
FRAG_DEV = 2
AXES = ("row", "col")
SPARE_VMEM = 10 * 1024 * 1024


def cycle_of(count):
    width = 1
    while (2 * width) ** 2 <= count:
        width *= 2
    depth = count // width
    walk = [(step, 0) for step in range(depth)]
    for turn, step in enumerate(range(depth - 1, -1, -1)):
        across = list(range(1, width))
        walk += [(step, place) for place in (across[::-1] if turn % 2 else across)]
    return [step * width + place for step, place in walk]


class Plan:
    def __init__(self, rows_here, cols_here):
        self.rows = lax.axis_size("row")
        self.cols = lax.axis_size("col")
        self.rows_here = rows_here
        self.cols_here = cols_here
        self.order = self.rows * rows_here
        self.block_rows = rows_here // BLK
        self.block_cols = cols_here // BLK
        self.cycle = cycle_of(self.cols)
        self.far = self.cols // 2

    def ring(self, value, to_partner=False):
        pairs = []
        for row in range(self.rows):
            direction = -1 if row % 2 else 1
            target_row = row ^ 1 if to_partner else row
            for place in range(self.cols):
                source = self.cycle[place]
                target = self.cycle[(place + direction) % self.cols]
                pairs.append((row * self.cols + source, target_row * self.cols + target))
        return lax.ppermute(value, AXES, pairs)

    def across(self, value, other):
        return lax.ppermute(value, "row", [(i, i ^ other) for i in range(self.rows)])

    def origin_first(self, distance, behind):
        col = lax.axis_index("col")
        forward = (lax.axis_index("row") % 2 == 0) == behind
        origin = jnp.int32(0)
        for place in range(self.cols):
            before = self.cycle[(place - distance) % self.cols]
            after = self.cycle[(place + distance) % self.cols]
            source = jnp.where(forward, jnp.int32(before), jnp.int32(after))
            origin = jnp.where(col == self.cycle[place], source, origin)
        return pl.multiple_of(origin * self.cols_here, self.cols_here)

    def row_first(self, other):
        return pl.multiple_of((lax.axis_index("row") ^ other) * self.rows_here, self.rows_here)


def masked(plan, band_ref, value):
    lines = []
    for i in range(plan.block_rows):
        line = []
        for j in range(plan.block_cols):
            row = lax.axis_index("row") * plan.block_rows + i
            col = lax.axis_index("col") * plan.block_cols + j
            keep = jnp.abs(row - col) <= jnp.maximum(band_ref[row], band_ref[col])
            block = value[i * BLK : (i + 1) * BLK, j * BLK : (j + 1) * BLK]
            line.append(block * keep.astype(jnp.float32))
        lines.append(jnp.concatenate(line, axis=1))
    return jnp.concatenate(lines, axis=0)


def dot(left, right):
    return jnp.dot(left, right, preferred_element_type=jnp.float32)


def call(kernel, outs, scalars, arrays, aliases=None):
    vmem = pl.BlockSpec(memory_space=pltpu.VMEM)
    smem = pl.BlockSpec(memory_space=pltpu.SMEM)
    moved = sum(a.size * a.dtype.itemsize for a in list(arrays) + list(outs))
    return pl.pallas_call(
        kernel,
        out_shape=outs,
        in_specs=[smem] * len(scalars) + [vmem] * len(arrays),
        out_specs=[vmem] * len(outs),
        input_output_aliases=aliases or {},
        compiler_params=pltpu.CompilerParams(vmem_limit_bytes=moved + SPARE_VMEM),
        cost_estimate=pl.CostEstimate(flops=0, bytes_accessed=0, transcendentals=0),
    )(*scalars, *arrays)


def lay_masked(plan, band_ref, to_ref, from_ref, row_first, col_first, to_row, to_col):
    for i in range(plan.block_rows):
        for j in range(plan.block_cols):
            row, col = row_first // BLK + i, col_first // BLK + j
            keep = jnp.abs(row - col) <= jnp.maximum(band_ref[row], band_ref[col])
            block = from_ref[i * BLK : (i + 1) * BLK, j * BLK : (j + 1) * BLK]
            lines = pl.ds(pl.multiple_of(to_row + i * BLK, BLK), BLK)
            lanes = pl.ds(pl.multiple_of(to_col + j * BLK, BLK), BLK)
            to_ref[lines, lanes] = block * keep.astype(jnp.bfloat16)


def near_places(plan, first, last):
    return [(distance, behind) for distance in range(first, last) for behind in ((True, False) if distance else (True,))]


def start_terms(plan, places, band_ref, right_ref, slab_ref, lefts):
    total = None
    for (distance, behind), left in zip(places, lefts):
        first = plan.origin_first(distance, behind)
        lay_masked(plan, band_ref, slab_ref, left, plan.row_first(0), first, 0, first)
        lanes = pl.ds(first, plan.cols_here)
        term = dot(slab_ref[:, lanes], right_ref[lanes, :])
        total = term if total is None else total + term
    return total


def start_kernel(plan, places, band_ref, *refs):
    rights, refs = refs[: plan.rows], refs[plan.rows :]
    *lefts, total_ref, right_ref, slab_ref = refs
    col_first = plan.origin_first(0, True)
    for other in range(plan.rows):
        row_first = plan.row_first(other)
        lay_masked(plan, band_ref, right_ref, rights[other], row_first, col_first, row_first, 0)
    total_ref[...] = start_terms(plan, places, band_ref, right_ref, slab_ref, lefts)


def square_kernel(plan, places, band_ref, before_ref, right_ref, _, far_ref, out_ref, slab_ref):
    total = before_ref[...] + start_terms(plan, places, band_ref, right_ref, slab_ref, [far_ref])
    out_ref[...] = masked(plan, band_ref, total).astype(jnp.bfloat16)


def pass_kernel(*refs):
    for from_ref, to_ref in zip(refs, refs[len(refs) // 2 :]):
        to_ref[:16, :BLK] = from_ref[:16, :BLK]


def near_kernel(plan, places, *refs):
    rights, refs = refs[: plan.rows], refs[plan.rows :]
    *lefts, total_ref, right_ref = refs
    for other in range(plan.rows):
        right_ref[pl.ds(plan.row_first(other), plan.rows_here), :] = rights[other][...]
    total = None
    for (distance, behind), left in zip(places, lefts):
        first = plan.origin_first(distance, behind)
        term = dot(left[...], right_ref[pl.ds(first, plan.cols_here), :])
        total = term if total is None else total + term
    total_ref[...] = total


def slab_terms(plan, slab_ref, pieces):
    total = None
    for other, piece in pieces:
        term = dot(slab_ref[:, pl.ds(plan.row_first(other), plan.rows_here)], piece[...])
        total = term if total is None else total + term
    return total


def some_kernel(plan, others, slab_ref, *refs):
    *pieces, total_ref = refs
    total_ref[...] = slab_terms(plan, slab_ref, list(zip(others, pieces)))


def more_kernel(plan, others, slab_ref, before_ref, *refs):
    *pieces, total_ref = refs
    total_ref[...] = before_ref[...] + slab_terms(plan, slab_ref, list(zip(others, pieces)))


def sign_kernel(plan, others, band_ref, slab_ref, total_ref, *refs):
    *pieces, sign_ref, density_ref = refs
    cubic = total_ref[...] + slab_terms(plan, slab_ref, list(zip(others, pieces)))
    start = slab_ref[:, pl.ds(plan.origin_first(0, True), plan.cols_here)].astype(jnp.float32)
    sign = masked(plan, band_ref, 1.5 * start - 0.5 * cubic).astype(jnp.bfloat16)
    sign_ref[...] = sign
    first_row = lax.axis_index("row") * plan.rows_here
    first_col = lax.axis_index("col") * plan.cols_here
    rows = first_row + lax.broadcasted_iota(jnp.int32, sign.shape, 0)
    cols = first_col + lax.broadcasted_iota(jnp.int32, sign.shape, 1)
    identity = (rows == cols).astype(jnp.float32)
    density_ref[...] = (0.5 * (identity - sign.astype(jnp.float32))).astype(jnp.bfloat16)


def weighted_kernel(plan, others, band_ref, slab_ref, *refs):
    *pieces, out_ref = refs
    total = slab_terms(plan, slab_ref, list(zip(others, pieces)))
    out_ref[...] = masked(plan, band_ref, total).astype(jnp.bfloat16)


def energy_kernel(plan, places, band_ref, frag_ref, total_ref, right_ref, deriv_ref, *refs):
    *lefts, energy_ref, sums_ref = refs
    total = total_ref[...]
    for (distance, behind), left in zip(places, lefts):
        first = plan.origin_first(distance, behind)
        total = total + dot(left[...], right_ref[pl.ds(first, plan.cols_here), :])
    energy = masked(plan, band_ref, total).astype(jnp.bfloat16)
    energy_ref[...] = energy
    weighed = energy.astype(jnp.float32) * deriv_ref[...].astype(jnp.float32)
    terms = jnp.sum(weighed, axis=0, keepdims=True)
    count = FRAG_DEV * plan.cols
    fragment = lax.broadcasted_iota(jnp.int32, (count, BLK), 0)
    sums = jnp.zeros((count, BLK), jnp.float32)
    for j in range(plan.block_cols):
        owner = frag_ref[lax.axis_index("col") * plan.block_cols + j]
        line = jnp.broadcast_to(terms[:, j * BLK : (j + 1) * BLK], (count, BLK))
        sums = sums + jnp.where(fragment == owner, line, 0.0)
    sums_ref[...] = sums


def body(ham, deriv, band, frag_of):
    plan = Plan(*ham.shape)
    bind = functools.partial
    block = jax.ShapeDtypeStruct(ham.shape, jnp.bfloat16)
    total_type = jax.ShapeDtypeStruct(ham.shape, jnp.float32)
    slab_type = jax.ShapeDtypeStruct((plan.rows_here, plan.order), jnp.bfloat16)
    column_type = jax.ShapeDtypeStruct((plan.order, plan.cols_here), jnp.bfloat16)
    others = range(plan.rows)

    def exchange_start(value):
        return [plan.across(value, other) for other in range(2, plan.rows, 2)]

    def exchange_end(first_two, crossed):
        return list(first_two) + [piece for value in crossed for piece in (value, plan.across(value, 1))]

    def gather(mine, partner, hand_over):
        shards = [mine]
        for distance in range(1, plan.far):
            mine = plan.ring(mine)
            last = distance == plan.far - 1 and not hand_over
            partner = plan.ring(partner, last)
            shards += [mine, partner if last else plan.across(partner, 1)]
        return shards, plan.ring(mine)

    partner = plan.across(ham, 1)
    shards, far = gather(ham, partner, False)
    column = exchange_end([ham, partner], exchange_start(ham))
    total, right, slab = call(
        bind(start_kernel, plan, near_places(plan, 0, plan.far)),
        [total_type, column_type, slab_type],
        [band],
        column + shards,
    )
    square, slab = call(
        bind(square_kernel, plan, [(plan.far, True)]), [block, slab_type], [band], [total, right, slab, far], {3: 1}
    )

    crossed = exchange_start(square)
    partner = plan.across(square, 1)
    (total,) = call(bind(some_kernel, plan, [0, 1]), [total_type], [], [slab, square, partner])
    *crossed, total = lax.optimization_barrier((*crossed, total))
    column = exchange_end([square, partner], crossed)
    even, odd = list(others)[2::2], list(others)[3::2]
    (total,) = call(bind(more_kernel, plan, even), [total_type], [], [slab, total] + column[2::2])
    sign_iterate, density = call(
        bind(sign_kernel, plan, odd), [block, block], [band], [slab, total] + column[3::2]
    )

    partner = plan.across(density, 1)
    shards, far = gather(density, partner, True)
    column = exchange_end([density, partner], exchange_start(density))
    (weighted,) = call(bind(weighted_kernel, plan, others), [block], [band], [slab] + column)
    column = exchange_end([weighted, plan.across(weighted, 1)], exchange_start(weighted))
    places = near_places(plan, 0, plan.far)
    late = [shards[-1], far]
    total, right = call(bind(near_kernel, plan, places[:-1]), [total_type, column_type], [], column + shards[:-1])
    energy_density, sums = call(
        bind(energy_kernel, plan, places[-1:] + [(plan.far, True)]),
        [block, jax.ShapeDtypeStruct((FRAG_DEV * plan.cols, BLK), jnp.float32)],
        [band, frag_of],
        [total, right, deriv] + late,
    )
    sums = sums.reshape(1, plan.cols, FRAG_DEV, BLK)
    sums = jnp.broadcast_to(sums, (plan.rows, plan.cols, FRAG_DEV, BLK))
    sums = sums.reshape(plan.rows * plan.cols, FRAG_DEV, BLK)
    pulay_terms = jnp.sum(lax.all_to_all(sums, AXES, 0, 0), axis=0)
    return (sign_iterate, energy_density, pulay_terms)


def solution(mesh):
    placed = (P("row", "col"), P("row", "col"), P(), P())
    return jax.shard_map(
        body,
        mesh=mesh,
        in_specs=placed,
        out_specs=(P("row", "col"), P("row", "col"), P("col", None)),
        check_vma=False,
    )
```

```python
import functools

import jax
import jax.numpy as jnp
from jax import lax
from jax.experimental import pallas as pl
from jax.experimental.pallas import tpu as pltpu
from jax.sharding import PartitionSpec as P

BLK = 128
FRAG_DEV = 2
AXES = ("row", "col")
SPARE_VMEM = 10 * 1024 * 1024


def cycle_of(count):
    width = 1
    while (2 * width) ** 2 <= count:
        width *= 2
    depth = count // width
    walk = [(step, 0) for step in range(depth)]
    for turn, step in enumerate(range(depth - 1, -1, -1)):
        across = list(range(1, width))
        walk += [(step, place) for place in (across[::-1] if turn % 2 else across)]
    return [step * width + place for step, place in walk]


class Plan:
    def __init__(self, rows_here, cols_here):
        self.rows = lax.axis_size("row")
        self.cols = lax.axis_size("col")
        self.rows_here = rows_here
        self.cols_here = cols_here
        self.order = self.rows * rows_here
        self.block_rows = rows_here // BLK
        self.block_cols = cols_here // BLK
        self.cycle = cycle_of(self.cols)
        self.far = self.cols // 2

    def ring(self, value, to_partner=False):
        pairs = []
        for row in range(self.rows):
            direction = -1 if row % 2 else 1
            target_row = row ^ 1 if to_partner else row
            for place in range(self.cols):
                source = self.cycle[place]
                target = self.cycle[(place + direction) % self.cols]
                pairs.append((row * self.cols + source, target_row * self.cols + target))
        return lax.ppermute(value, AXES, pairs)

    def across(self, value, other):
        return lax.ppermute(value, "row", [(i, i ^ other) for i in range(self.rows)])

    def origin_first(self, distance, behind):
        col = lax.axis_index("col")
        forward = (lax.axis_index("row") % 2 == 0) == behind
        origin = jnp.int32(0)
        for place in range(self.cols):
            before = self.cycle[(place - distance) % self.cols]
            after = self.cycle[(place + distance) % self.cols]
            source = jnp.where(forward, jnp.int32(before), jnp.int32(after))
            origin = jnp.where(col == self.cycle[place], source, origin)
        return pl.multiple_of(origin * self.cols_here, self.cols_here)

    def row_first(self, other):
        return pl.multiple_of((lax.axis_index("row") ^ other) * self.rows_here, self.rows_here)


def masked(plan, band_ref, value):
    lines = []
    for i in range(plan.block_rows):
        line = []
        for j in range(plan.block_cols):
            row = lax.axis_index("row") * plan.block_rows + i
            col = lax.axis_index("col") * plan.block_cols + j
            keep = jnp.abs(row - col) <= jnp.maximum(band_ref[row], band_ref[col])
            block = value[i * BLK : (i + 1) * BLK, j * BLK : (j + 1) * BLK]
            line.append(block * keep.astype(jnp.float32))
        lines.append(jnp.concatenate(line, axis=1))
    return jnp.concatenate(lines, axis=0)


def dot(left, right):
    return jnp.dot(left, right, preferred_element_type=jnp.float32)


def call(kernel, outs, scalars, arrays, aliases=None):
    vmem = pl.BlockSpec(memory_space=pltpu.VMEM)
    smem = pl.BlockSpec(memory_space=pltpu.SMEM)
    moved = sum(a.size * a.dtype.itemsize for a in list(arrays) + list(outs))
    return pl.pallas_call(
        kernel,
        out_shape=outs,
        in_specs=[smem] * len(scalars) + [vmem] * len(arrays),
        out_specs=[vmem] * len(outs),
        input_output_aliases=aliases or {},
        compiler_params=pltpu.CompilerParams(vmem_limit_bytes=moved + SPARE_VMEM),
        cost_estimate=pl.CostEstimate(flops=0, bytes_accessed=0, transcendentals=0),
    )(*scalars, *arrays)


def lay_masked(plan, band_ref, to_ref, from_ref, row_first, col_first, to_row, to_col):
    for i in range(plan.block_rows):
        for j in range(plan.block_cols):
            row, col = row_first // BLK + i, col_first // BLK + j
            keep = jnp.abs(row - col) <= jnp.maximum(band_ref[row], band_ref[col])
            block = from_ref[i * BLK : (i + 1) * BLK, j * BLK : (j + 1) * BLK]
            lines = pl.ds(pl.multiple_of(to_row + i * BLK, BLK), BLK)
            lanes = pl.ds(pl.multiple_of(to_col + j * BLK, BLK), BLK)
            to_ref[lines, lanes] = block * keep.astype(jnp.bfloat16)


def near_places(plan, first, last):
    return [(distance, behind) for distance in range(first, last) for behind in ((True, False) if distance else (True,))]


def start_terms(plan, places, band_ref, right_ref, slab_ref, lefts):
    total = None
    for (distance, behind), left in zip(places, lefts):
        first = plan.origin_first(distance, behind)
        lay_masked(plan, band_ref, slab_ref, left, plan.row_first(0), first, 0, first)
        lanes = pl.ds(first, plan.cols_here)
        term = dot(slab_ref[:, lanes], right_ref[lanes, :])
        total = term if total is None else total + term
    return total


def start_kernel(plan, places, band_ref, *refs):
    rights, refs = refs[: plan.rows], refs[plan.rows :]
    *lefts, total_ref, right_ref, slab_ref = refs
    col_first = plan.origin_first(0, True)
    for other in range(plan.rows):
        row_first = plan.row_first(other)
        lay_masked(plan, band_ref, right_ref, rights[other], row_first, col_first, row_first, 0)
    total_ref[...] = start_terms(plan, places, band_ref, right_ref, slab_ref, lefts)


def square_kernel(plan, places, band_ref, before_ref, right_ref, _, far_ref, out_ref, slab_ref):
    total = before_ref[...] + start_terms(plan, places, band_ref, right_ref, slab_ref, [far_ref])
    out_ref[...] = masked(plan, band_ref, total).astype(jnp.bfloat16)


def pass_kernel(*refs):
    for from_ref, to_ref in zip(refs, refs[len(refs) // 2 :]):
        to_ref[:16, :BLK] = from_ref[:16, :BLK]


def near_kernel(plan, places, *refs):
    rights, refs = refs[: plan.rows], refs[plan.rows :]
    *lefts, total_ref, right_ref = refs
    for other in range(plan.rows):
        right_ref[pl.ds(plan.row_first(other), plan.rows_here), :] = rights[other][...]
    total = None
    for (distance, behind), left in zip(places, lefts):
        first = plan.origin_first(distance, behind)
        term = dot(left[...], right_ref[pl.ds(first, plan.cols_here), :])
        total = term if total is None else total + term
    total_ref[...] = total


def slab_terms(plan, slab_ref, pieces):
    total = None
    for other, piece in pieces:
        term = dot(slab_ref[:, pl.ds(plan.row_first(other), plan.rows_here)], piece[...])
        total = term if total is None else total + term
    return total


def some_kernel(plan, others, slab_ref, *refs):
    *pieces, total_ref = refs
    total_ref[...] = slab_terms(plan, slab_ref, list(zip(others, pieces)))


def more_kernel(plan, others, slab_ref, before_ref, *refs):
    *pieces, total_ref = refs
    total_ref[...] = before_ref[...] + slab_terms(plan, slab_ref, list(zip(others, pieces)))


def sign_kernel(plan, others, band_ref, slab_ref, total_ref, *refs):
    *pieces, sign_ref, density_ref = refs
    cubic = total_ref[...] + slab_terms(plan, slab_ref, list(zip(others, pieces)))
    start = slab_ref[:, pl.ds(plan.origin_first(0, True), plan.cols_here)].astype(jnp.float32)
    sign = masked(plan, band_ref, 1.5 * start - 0.5 * cubic).astype(jnp.bfloat16)
    sign_ref[...] = sign
    first_row = lax.axis_index("row") * plan.rows_here
    first_col = lax.axis_index("col") * plan.cols_here
    rows = first_row + lax.broadcasted_iota(jnp.int32, sign.shape, 0)
    cols = first_col + lax.broadcasted_iota(jnp.int32, sign.shape, 1)
    identity = (rows == cols).astype(jnp.float32)
    density_ref[...] = (0.5 * (identity - sign.astype(jnp.float32))).astype(jnp.bfloat16)


def weighted_kernel(plan, others, band_ref, slab_ref, before_ref, *refs):
    *pieces, out_ref = refs
    total = before_ref[...] + slab_terms(plan, slab_ref, list(zip(others, pieces)))
    out_ref[...] = masked(plan, band_ref, total).astype(jnp.bfloat16)


def energy_kernel(plan, places, band_ref, frag_ref, total_ref, right_ref, deriv_ref, *refs):
    *lefts, energy_ref, sums_ref = refs
    total = total_ref[...]
    for (distance, behind), left in zip(places, lefts):
        first = plan.origin_first(distance, behind)
        total = total + dot(left[...], right_ref[pl.ds(first, plan.cols_here), :])
    energy = masked(plan, band_ref, total).astype(jnp.bfloat16)
    energy_ref[...] = energy
    weighed = energy.astype(jnp.float32) * deriv_ref[...].astype(jnp.float32)
    terms = jnp.sum(weighed, axis=0, keepdims=True)
    count = FRAG_DEV * plan.cols
    fragment = lax.broadcasted_iota(jnp.int32, (count, BLK), 0)
    sums = jnp.zeros((count, BLK), jnp.float32)
    for j in range(plan.block_cols):
        owner = frag_ref[lax.axis_index("col") * plan.block_cols + j]
        line = jnp.broadcast_to(terms[:, j * BLK : (j + 1) * BLK], (count, BLK))
        sums = sums + jnp.where(fragment == owner, line, 0.0)
    sums_ref[...] = sums


def body(ham, deriv, band, frag_of):
    plan = Plan(*ham.shape)
    bind = functools.partial
    block = jax.ShapeDtypeStruct(ham.shape, jnp.bfloat16)
    total_type = jax.ShapeDtypeStruct(ham.shape, jnp.float32)
    slab_type = jax.ShapeDtypeStruct((plan.rows_here, plan.order), jnp.bfloat16)
    column_type = jax.ShapeDtypeStruct((plan.order, plan.cols_here), jnp.bfloat16)
    others = range(plan.rows)

    def exchange_start(value):
        return [plan.across(value, other) for other in range(2, plan.rows, 2)]

    def exchange_end(first_two, crossed):
        return list(first_two) + [piece for value in crossed for piece in (value, plan.across(value, 1))]

    def gather(mine, partner, hand_over):
        shards = [mine]
        for distance in range(1, plan.far):
            mine = plan.ring(mine)
            last = distance == plan.far - 1 and not hand_over
            partner = plan.ring(partner, last)
            shards += [mine, partner if last else plan.across(partner, 1)]
        return shards, plan.ring(mine)

    partner = plan.across(ham, 1)
    shards, far = gather(ham, partner, False)
    column = exchange_end([ham, partner], exchange_start(ham))
    total, right, slab = call(
        bind(start_kernel, plan, near_places(plan, 0, plan.far)),
        [total_type, column_type, slab_type],
        [band],
        column + shards,
    )
    square, slab = call(
        bind(square_kernel, plan, [(plan.far, True)]), [block, slab_type], [band], [total, right, slab, far], {3: 1}
    )

    crossed = exchange_start(square)
    partner = plan.across(square, 1)
    (total,) = call(bind(some_kernel, plan, [0, 1]), [total_type], [], [slab, square, partner])
    *crossed, total = lax.optimization_barrier((*crossed, total))
    column = exchange_end([square, partner], crossed)
    even, odd = list(others)[2::2], list(others)[3::2]
    (total,) = call(bind(more_kernel, plan, even), [total_type], [], [slab, total] + column[2::2])
    sign_iterate, density = call(
        bind(sign_kernel, plan, odd), [block, block], [band], [slab, total] + column[3::2]
    )

    partner = plan.across(density, 1)
    shards, far = gather(density, partner, True)
    column = exchange_end([density, partner], exchange_start(density))
    (total,) = call(bind(some_kernel, plan, [0, 1]), [total_type], [], [slab] + column[:2])
    (total,) = call(bind(more_kernel, plan, even), [total_type], [], [slab, total] + column[2::2])
    (weighted,) = call(bind(weighted_kernel, plan, odd), [block], [band], [slab, total] + column[3::2])
    column = exchange_end([weighted, plan.across(weighted, 1)], exchange_start(weighted))
    places = near_places(plan, 0, plan.far)
    late = [shards[-1], far]
    total, right = call(bind(near_kernel, plan, places[:-1]), [total_type, column_type], [], column + shards[:-1])
    energy_density, sums = call(
        bind(energy_kernel, plan, places[-1:] + [(plan.far, True)]),
        [block, jax.ShapeDtypeStruct((FRAG_DEV * plan.cols, BLK), jnp.float32)],
        [band, frag_of],
        [total, right, deriv] + late,
    )
    sums = sums.reshape(1, plan.cols, FRAG_DEV, BLK)
    sums = jnp.broadcast_to(sums, (plan.rows, plan.cols, FRAG_DEV, BLK))
    sums = sums.reshape(plan.rows * plan.cols, FRAG_DEV, BLK)
    pulay_terms = jnp.sum(lax.all_to_all(sums, AXES, 0, 0), axis=0)
    return (sign_iterate, energy_density, pulay_terms)


def solution(mesh):
    placed = (P("row", "col"), P("row", "col"), P(), P())
    return jax.shard_map(
        body,
        mesh=mesh,
        in_specs=placed,
        out_specs=(P("row", "col"), P("row", "col"), P("col", None)),
        check_vma=False,
    )
```

```python
import functools

import jax
import jax.numpy as jnp
from jax import lax
from jax.experimental import pallas as pl
from jax.experimental.pallas import tpu as pltpu
from jax.sharding import PartitionSpec as P

BLK = 128
FRAG_DEV = 2
AXES = ("row", "col")
SPAN = 1
SPARE_VMEM = 10 * 1024 * 1024


def cycle_of(count):
    width = 1
    while (2 * width) ** 2 <= count:
        width *= 2
    depth = count // width
    walk = [(step, 0) for step in range(depth)]
    for turn, step in enumerate(range(depth - 1, -1, -1)):
        across = list(range(1, width))
        walk += [(step, place) for place in (across[::-1] if turn % 2 else across)]
    return [step * width + place for step, place in walk]


class Plan:
    def __init__(self, rows_here, cols_here):
        self.rows = lax.axis_size("row")
        self.cols = lax.axis_size("col")
        self.rows_here = rows_here
        self.cols_here = cols_here
        self.order = self.rows * rows_here
        self.block_rows = rows_here // BLK
        self.block_cols = cols_here // BLK
        self.cycle = cycle_of(self.cols)
        self.far = self.cols // 2

    def ring(self, value, to_partner=False):
        pairs = []
        for row in range(self.rows):
            direction = -1 if row % 2 else 1
            target_row = row ^ 1 if to_partner else row
            for place in range(self.cols):
                source = self.cycle[place]
                target = self.cycle[(place + direction) % self.cols]
                pairs.append((row * self.cols + source, target_row * self.cols + target))
        return lax.ppermute(value, AXES, pairs)

    def across(self, value, other):
        return lax.ppermute(value, "row", [(i, i ^ other) for i in range(self.rows)])

    def origin_first(self, distance, behind):
        col = lax.axis_index("col")
        forward = (lax.axis_index("row") % 2 == 0) == behind
        origin = jnp.int32(0)
        for place in range(self.cols):
            before = self.cycle[(place - distance) % self.cols]
            after = self.cycle[(place + distance) % self.cols]
            source = jnp.where(forward, jnp.int32(before), jnp.int32(after))
            origin = jnp.where(col == self.cycle[place], source, origin)
        return pl.multiple_of(origin * self.cols_here, self.cols_here)

    def row_first(self, other):
        return pl.multiple_of((lax.axis_index("row") ^ other) * self.rows_here, self.rows_here)


def spans(plan):
    step = min(SPAN, plan.block_rows)
    return [(i, slice(i * BLK, min(i + step, plan.block_rows) * BLK)) for i in range(0, plan.block_rows, step)]


def masked(plan, band_ref, value, first_block):
    lines = []
    for i in range(value.shape[0] // BLK):
        line = []
        for j in range(plan.block_cols):
            row = lax.axis_index("row") * plan.block_rows + first_block + i
            col = lax.axis_index("col") * plan.block_cols + j
            keep = jnp.abs(row - col) <= jnp.maximum(band_ref[row], band_ref[col])
            block = value[i * BLK : (i + 1) * BLK, j * BLK : (j + 1) * BLK]
            line.append(block * keep.astype(jnp.float32))
        lines.append(jnp.concatenate(line, axis=1))
    return jnp.concatenate(lines, axis=0)


def dot(left, right):
    return jnp.dot(left, right, preferred_element_type=jnp.float32)


def call(kernel, outs, scalars, arrays, aliases=None):
    vmem = pl.BlockSpec(memory_space=pltpu.VMEM)
    smem = pl.BlockSpec(memory_space=pltpu.SMEM)
    moved = sum(a.size * a.dtype.itemsize for a in list(arrays) + list(outs))
    return pl.pallas_call(
        kernel,
        out_shape=outs,
        in_specs=[smem] * len(scalars) + [vmem] * len(arrays),
        out_specs=[vmem] * len(outs),
        input_output_aliases=aliases or {},
        compiler_params=pltpu.CompilerParams(vmem_limit_bytes=moved + SPARE_VMEM),
        cost_estimate=pl.CostEstimate(flops=0, bytes_accessed=0, transcendentals=0),
    )(*scalars, *arrays)


def lay_masked(plan, band_ref, to_ref, from_ref, row_first, col_first, to_row, to_col):
    for i in range(plan.block_rows):
        for j in range(plan.block_cols):
            row, col = row_first // BLK + i, col_first // BLK + j
            keep = jnp.abs(row - col) <= jnp.maximum(band_ref[row], band_ref[col])
            block = from_ref[i * BLK : (i + 1) * BLK, j * BLK : (j + 1) * BLK]
            lines = pl.ds(pl.multiple_of(to_row + i * BLK, BLK), BLK)
            lanes = pl.ds(pl.multiple_of(to_col + j * BLK, BLK), BLK)
            to_ref[lines, lanes] = block * keep.astype(jnp.bfloat16)


def near_places(plan, first, last):
    return [(distance, behind) for distance in range(first, last) for behind in ((True, False) if distance else (True,))]


def start_terms(plan, places, band_ref, right_ref, slab_ref, lefts):
    total = None
    for (distance, behind), left in zip(places, lefts):
        first = plan.origin_first(distance, behind)
        lay_masked(plan, band_ref, slab_ref, left, plan.row_first(0), first, 0, first)
        lanes = pl.ds(first, plan.cols_here)
        term = dot(slab_ref[:, lanes], right_ref[lanes, :])
        total = term if total is None else total + term
    return total


def start_kernel(plan, places, band_ref, *refs):
    rights, refs = refs[: plan.rows], refs[plan.rows :]
    *lefts, total_ref, right_ref, slab_ref = refs
    col_first = plan.origin_first(0, True)
    for other in range(plan.rows):
        row_first = plan.row_first(other)
        lay_masked(plan, band_ref, right_ref, rights[other], row_first, col_first, row_first, 0)
    total_ref[...] = start_terms(plan, places, band_ref, right_ref, slab_ref, lefts)


def square_kernel(plan, band_ref, before_ref, right_ref, _, far_ref, out_ref, slab_ref):
    first = plan.origin_first(plan.far, True)
    lanes = pl.ds(first, plan.cols_here)
    lay_masked(plan, band_ref, slab_ref, far_ref, plan.row_first(0), first, 0, first)
    for block, lines in spans(plan):
        total = before_ref[lines, :] + dot(slab_ref[lines, lanes], right_ref[lanes, :])
        out_ref[lines, :] = masked(plan, band_ref, total, block).astype(jnp.bfloat16)


def near_kernel(plan, places, *refs):
    rights, refs = refs[: plan.rows], refs[plan.rows :]
    *lefts, total_ref, right_ref = refs
    for other in range(plan.rows):
        right_ref[pl.ds(plan.row_first(other), plan.rows_here), :] = rights[other][...]
    total = None
    for (distance, behind), left in zip(places, lefts):
        first = plan.origin_first(distance, behind)
        term = dot(left[...], right_ref[pl.ds(first, plan.cols_here), :])
        total = term if total is None else total + term
    total_ref[...] = total


def slab_terms(plan, slab_ref, pieces, lines=slice(None)):
    total = None
    for other, piece in pieces:
        term = dot(slab_ref[lines, pl.ds(plan.row_first(other), plan.rows_here)], piece[...])
        total = term if total is None else total + term
    return total


def some_kernel(plan, others, slab_ref, *refs):
    *pieces, total_ref = refs
    total_ref[...] = slab_terms(plan, slab_ref, list(zip(others, pieces)))


def more_kernel(plan, others, slab_ref, before_ref, *refs):
    *pieces, total_ref = refs
    total_ref[...] = before_ref[...] + slab_terms(plan, slab_ref, list(zip(others, pieces)))


def sign_kernel(plan, others, band_ref, slab_ref, total_ref, *refs):
    *pieces, sign_ref, density_ref = refs
    first_row = lax.axis_index("row") * plan.rows_here
    first_col = plan.origin_first(0, True)
    for block, lines in spans(plan):
        cubic = total_ref[lines, :] + slab_terms(plan, slab_ref, list(zip(others, pieces)), lines)
        start = slab_ref[lines, pl.ds(first_col, plan.cols_here)].astype(jnp.float32)
        sign = masked(plan, band_ref, 1.5 * start - 0.5 * cubic, block).astype(jnp.bfloat16)
        sign_ref[lines, :] = sign
        rows = first_row + block * BLK + lax.broadcasted_iota(jnp.int32, sign.shape, 0)
        cols = first_col + lax.broadcasted_iota(jnp.int32, sign.shape, 1)
        identity = (rows == cols).astype(jnp.float32)
        density_ref[lines, :] = (0.5 * (identity - sign.astype(jnp.float32))).astype(jnp.bfloat16)


def copy_kernel(from_ref, to_ref):
    to_ref[...] = from_ref[...]


def weighted_kernel(plan, others, band_ref, slab_ref, before_ref, *refs):
    *pieces, out_ref = refs
    for block, lines in spans(plan):
        total = before_ref[lines, :] + slab_terms(plan, slab_ref, list(zip(others, pieces)), lines)
        out_ref[lines, :] = masked(plan, band_ref, total, block).astype(jnp.bfloat16)


def energy_kernel(plan, places, band_ref, frag_ref, total_ref, right_ref, deriv_ref, *refs):
    *lefts, energy_ref, sums_ref = refs
    terms = jnp.zeros((8, plan.cols_here), jnp.float32)
    for block, lines in spans(plan):
        total = total_ref[lines, :]
        for (distance, behind), left in zip(places, lefts):
            first = plan.origin_first(distance, behind)
            total = total + dot(left[lines, :], right_ref[pl.ds(first, plan.cols_here), :])
        energy = masked(plan, band_ref, total, block).astype(jnp.bfloat16)
        energy_ref[lines, :] = energy
        weighed = energy.astype(jnp.float32) * deriv_ref[lines, :].astype(jnp.float32)
        terms = terms + jnp.sum(weighed.reshape(-1, 8, plan.cols_here), axis=0)
    terms = jnp.sum(terms, axis=0, keepdims=True)
    count = FRAG_DEV * plan.cols
    fragment = lax.broadcasted_iota(jnp.int32, (count, BLK), 0)
    sums = jnp.zeros((count, BLK), jnp.float32)
    for j in range(plan.block_cols):
        owner = frag_ref[lax.axis_index("col") * plan.block_cols + j]
        line = jnp.broadcast_to(terms[:, j * BLK : (j + 1) * BLK], (count, BLK))
        sums = sums + jnp.where(fragment == owner, line, 0.0)
    sums_ref[...] = sums


def body(ham, deriv, band, frag_of):
    plan = Plan(*ham.shape)
    bind = functools.partial
    block = jax.ShapeDtypeStruct(ham.shape, jnp.bfloat16)
    total_type = jax.ShapeDtypeStruct(ham.shape, jnp.float32)
    slab_type = jax.ShapeDtypeStruct((plan.rows_here, plan.order), jnp.bfloat16)
    column_type = jax.ShapeDtypeStruct((plan.order, plan.cols_here), jnp.bfloat16)
    others = range(plan.rows)

    def exchange_start(value):
        return [plan.across(value, other) for other in range(2, plan.rows, 2)]

    def exchange_end(first_two, crossed):
        return list(first_two) + [piece for value in crossed for piece in (value, plan.across(value, 1))]

    def gather(mine, partner, hand_over):
        shards = [mine]
        for distance in range(1, plan.far):
            mine = plan.ring(mine)
            last = distance == plan.far - 1 and not hand_over
            partner = plan.ring(partner, last)
            shards += [mine, partner if last else plan.across(partner, 1)]
        return shards, plan.ring(mine)

    partner = plan.across(ham, 1)
    shards, far = gather(ham, partner, False)
    column = exchange_end([ham, partner], exchange_start(ham))
    total, right, slab = call(
        bind(start_kernel, plan, near_places(plan, 0, plan.far)),
        [total_type, column_type, slab_type],
        [band],
        column + shards,
    )
    square, slab = call(
        bind(square_kernel, plan), [block, slab_type], [band], [total, right, slab, far], {3: 1}
    )

    crossed = exchange_start(square)
    partner = plan.across(square, 1)
    (total,) = call(bind(some_kernel, plan, [0, 1]), [total_type], [], [slab, square, partner])
    *crossed, total = lax.optimization_barrier((*crossed, total))
    column = exchange_end([square, partner], crossed)
    even, odd = list(others)[2::2], list(others)[3::2]
    (total,) = call(bind(more_kernel, plan, even), [total_type], [], [slab, total] + column[2::2])
    sign, density = call(
        bind(sign_kernel, plan, odd), [block, block], [band], [slab, total] + column[3::2]
    )

    partner = plan.across(density, 1)
    shards, far = gather(density, partner, True)
    column = exchange_end([density, partner], exchange_start(density))
    (total,) = call(bind(some_kernel, plan, [0, 1]), [total_type], [], [slab] + column[:2])
    (total,) = call(bind(more_kernel, plan, even), [total_type], [], [slab, total] + column[2::2])
    (weighted,) = call(bind(weighted_kernel, plan, odd), [block], [band], [slab, total] + column[3::2])
    column = exchange_end([weighted, plan.across(weighted, 1)], exchange_start(weighted))
    (sign_iterate,) = call(copy_kernel, [block], [], [sign])
    shards[0], sign_iterate = lax.optimization_barrier((shards[0], sign_iterate))
    places = near_places(plan, 0, plan.far)
    late = [shards[-1], far]
    total, right = call(bind(near_kernel, plan, places[:-1]), [total_type, column_type], [], column + shards[:-1])
    energy_density, sums = call(
        bind(energy_kernel, plan, places[-1:] + [(plan.far, True)]),
        [block, jax.ShapeDtypeStruct((FRAG_DEV * plan.cols, BLK), jnp.float32)],
        [band, frag_of],
        [total, right, deriv] + late,
    )
    sums = sums.reshape(1, plan.cols, FRAG_DEV, BLK)
    sums = jnp.broadcast_to(sums, (plan.rows, plan.cols, FRAG_DEV, BLK))
    sums = sums.reshape(plan.rows * plan.cols, FRAG_DEV, BLK)
    pulay_terms = jnp.sum(lax.all_to_all(sums, AXES, 0, 0), axis=0)
    return (sign_iterate, energy_density, pulay_terms)


def solution(mesh):
    placed = (P("row", "col"), P("row", "col"), P(), P())
    return jax.shard_map(
        body,
        mesh=mesh,
        in_specs=placed,
        out_specs=(P("row", "col"), P("row", "col"), P("col", None)),
        check_vma=False,
    )
```

```python
import functools

import jax
import jax.numpy as jnp
from jax import lax
from jax.experimental import pallas as pl
from jax.experimental.pallas import tpu as pltpu
from jax.sharding import PartitionSpec as P

BLK = 128
FRAG_DEV = 2
AXES = ("row", "col")
SPAN = 1
SPARE_VMEM = 10 * 1024 * 1024


def cycle_of(count):
    width = 1
    while (2 * width) ** 2 <= count:
        width *= 2
    depth = count // width
    walk = [(step, 0) for step in range(depth)]
    for turn, step in enumerate(range(depth - 1, -1, -1)):
        across = list(range(1, width))
        walk += [(step, place) for place in (across[::-1] if turn % 2 else across)]
    return [step * width + place for step, place in walk]


class Plan:
    def __init__(self, rows_here, cols_here):
        self.rows = lax.axis_size("row")
        self.cols = lax.axis_size("col")
        self.rows_here = rows_here
        self.cols_here = cols_here
        self.order = self.rows * rows_here
        self.block_rows = rows_here // BLK
        self.block_cols = cols_here // BLK
        self.cycle = cycle_of(self.cols)
        self.far = self.cols // 2

    def ring(self, value, to_partner=False):
        pairs = []
        for row in range(self.rows):
            direction = -1 if row % 2 else 1
            target_row = row ^ 1 if to_partner else row
            for place in range(self.cols):
                source = self.cycle[place]
                target = self.cycle[(place + direction) % self.cols]
                pairs.append((row * self.cols + source, target_row * self.cols + target))
        return lax.ppermute(value, AXES, pairs)

    def across(self, value, other):
        return lax.ppermute(value, "row", [(i, i ^ other) for i in range(self.rows)])

    def origin_first(self, distance, behind):
        col = lax.axis_index("col")
        forward = (lax.axis_index("row") % 2 == 0) == behind
        origin = jnp.int32(0)
        for place in range(self.cols):
            before = self.cycle[(place - distance) % self.cols]
            after = self.cycle[(place + distance) % self.cols]
            source = jnp.where(forward, jnp.int32(before), jnp.int32(after))
            origin = jnp.where(col == self.cycle[place], source, origin)
        return pl.multiple_of(origin * self.cols_here, self.cols_here)

    def row_first(self, other):
        return pl.multiple_of((lax.axis_index("row") ^ other) * self.rows_here, self.rows_here)


def spans(plan):
    step = min(SPAN, plan.block_rows)
    return [(i, slice(i * BLK, min(i + step, plan.block_rows) * BLK)) for i in range(0, plan.block_rows, step)]


def masked(plan, band_ref, value, first_block):
    lines = []
    for i in range(value.shape[0] // BLK):
        line = []
        for j in range(plan.block_cols):
            row = lax.axis_index("row") * plan.block_rows + first_block + i
            col = lax.axis_index("col") * plan.block_cols + j
            keep = jnp.abs(row - col) <= jnp.maximum(band_ref[row], band_ref[col])
            block = value[i * BLK : (i + 1) * BLK, j * BLK : (j + 1) * BLK]
            line.append(block * keep.astype(jnp.float32))
        lines.append(jnp.concatenate(line, axis=1))
    return jnp.concatenate(lines, axis=0)


def dot(left, right):
    return jnp.dot(left, right, preferred_element_type=jnp.float32)


def call(kernel, outs, scalars, arrays, aliases=None):
    vmem = pl.BlockSpec(memory_space=pltpu.VMEM)
    smem = pl.BlockSpec(memory_space=pltpu.SMEM)
    moved = sum(a.size * a.dtype.itemsize for a in list(arrays) + list(outs))
    return pl.pallas_call(
        kernel,
        out_shape=outs,
        in_specs=[smem] * len(scalars) + [vmem] * len(arrays),
        out_specs=[vmem] * len(outs),
        input_output_aliases=aliases or {},
        compiler_params=pltpu.CompilerParams(vmem_limit_bytes=moved + SPARE_VMEM),
        cost_estimate=pl.CostEstimate(flops=0, bytes_accessed=0, transcendentals=0),
    )(*scalars, *arrays)


def lay_masked(plan, band_ref, to_ref, from_ref, row_first, col_first, to_row, to_col):
    for i in range(plan.block_rows):
        for j in range(plan.block_cols):
            row, col = row_first // BLK + i, col_first // BLK + j
            keep = jnp.abs(row - col) <= jnp.maximum(band_ref[row], band_ref[col])
            block = from_ref[i * BLK : (i + 1) * BLK, j * BLK : (j + 1) * BLK]
            lines = pl.ds(pl.multiple_of(to_row + i * BLK, BLK), BLK)
            lanes = pl.ds(pl.multiple_of(to_col + j * BLK, BLK), BLK)
            to_ref[lines, lanes] = block * keep.astype(jnp.bfloat16)


def near_places(plan, first, last):
    return [(distance, behind) for distance in range(first, last) for behind in ((True, False) if distance else (True,))]


def start_terms(plan, places, band_ref, right_ref, slab_ref, lefts):
    total = None
    for (distance, behind), left in zip(places, lefts):
        first = plan.origin_first(distance, behind)
        lay_masked(plan, band_ref, slab_ref, left, plan.row_first(0), first, 0, first)
        lanes = pl.ds(first, plan.cols_here)
        term = dot(slab_ref[:, lanes], right_ref[lanes, :])
        total = term if total is None else total + term
    return total


def start_kernel(plan, places, band_ref, *refs):
    rights, refs = refs[: plan.rows], refs[plan.rows :]
    *lefts, total_ref, right_ref, slab_ref = refs
    col_first = plan.origin_first(0, True)
    for other in range(plan.rows):
        row_first = plan.row_first(other)
        lay_masked(plan, band_ref, right_ref, rights[other], row_first, col_first, row_first, 0)
    total_ref[...] = start_terms(plan, places, band_ref, right_ref, slab_ref, lefts)


def square_kernel(plan, band_ref, before_ref, right_ref, _, far_ref, *refs):
    *out_refs, slab_ref = refs
    first = plan.origin_first(plan.far, True)
    lanes = pl.ds(first, plan.cols_here)
    lay_masked(plan, band_ref, slab_ref, far_ref, plan.row_first(0), first, 0, first)
    half = plan.block_rows // 2
    for block in range(plan.block_rows):
        lines = slice(block * BLK, (block + 1) * BLK)
        total = before_ref[lines, :] + dot(slab_ref[lines, lanes], right_ref[lanes, :])
        place = slice(block % half * BLK, (block % half + 1) * BLK)
        out_refs[block // half][place, :] = masked(plan, band_ref, total, block).astype(jnp.bfloat16)


def near_kernel(plan, places, *refs):
    rights, refs = refs[: plan.rows], refs[plan.rows :]
    *lefts, total_ref, right_ref = refs
    for other in range(plan.rows):
        right_ref[pl.ds(plan.row_first(other), plan.rows_here), :] = rights[other][...]
    total = None
    for (distance, behind), left in zip(places, lefts):
        first = plan.origin_first(distance, behind)
        term = dot(left[...], right_ref[pl.ds(first, plan.cols_here), :])
        total = term if total is None else total + term
    total_ref[...] = total


def slab_terms(plan, slab_ref, pieces, lines=slice(None)):
    total = None
    for (other, part), piece in pieces:
        count = piece.shape[0]
        first = pl.multiple_of(plan.row_first(other) + part * count, count)
        term = dot(slab_ref[lines, pl.ds(first, count)], piece[...])
        total = term if total is None else total + term
    return total


def some_kernel(plan, others, slab_ref, *refs):
    *pieces, total_ref = refs
    total_ref[...] = slab_terms(plan, slab_ref, list(zip(others, pieces)))


def more_kernel(plan, others, slab_ref, before_ref, *refs):
    *pieces, total_ref = refs
    total_ref[...] = before_ref[...] + slab_terms(plan, slab_ref, list(zip(others, pieces)))


def sign_kernel(plan, others, band_ref, slab_ref, total_ref, *refs):
    *pieces, sign_ref, density_ref = refs
    first_row = lax.axis_index("row") * plan.rows_here
    first_col = plan.origin_first(0, True)
    for block, lines in spans(plan):
        cubic = total_ref[lines, :] + slab_terms(plan, slab_ref, list(zip(others, pieces)), lines)
        start = slab_ref[lines, pl.ds(first_col, plan.cols_here)].astype(jnp.float32)
        sign = masked(plan, band_ref, 1.5 * start - 0.5 * cubic, block).astype(jnp.bfloat16)
        sign_ref[lines, :] = sign
        rows = first_row + block * BLK + lax.broadcasted_iota(jnp.int32, sign.shape, 0)
        cols = first_col + lax.broadcasted_iota(jnp.int32, sign.shape, 1)
        identity = (rows == cols).astype(jnp.float32)
        density_ref[lines, :] = (0.5 * (identity - sign.astype(jnp.float32))).astype(jnp.bfloat16)


def copy_kernel(from_ref, to_ref):
    to_ref[...] = from_ref[...]


def weighted_kernel(plan, others, band_ref, slab_ref, before_ref, *refs):
    *pieces, out_ref = refs
    for block, lines in spans(plan):
        total = before_ref[lines, :] + slab_terms(plan, slab_ref, list(zip(others, pieces)), lines)
        out_ref[lines, :] = masked(plan, band_ref, total, block).astype(jnp.bfloat16)


def energy_kernel(plan, places, band_ref, frag_ref, total_ref, right_ref, deriv_ref, *refs):
    *lefts, energy_ref, sums_ref = refs
    terms = jnp.zeros((8, plan.cols_here), jnp.float32)
    for block, lines in spans(plan):
        total = total_ref[lines, :]
        for (distance, behind), left in zip(places, lefts):
            first = plan.origin_first(distance, behind)
            total = total + dot(left[lines, :], right_ref[pl.ds(first, plan.cols_here), :])
        energy = masked(plan, band_ref, total, block).astype(jnp.bfloat16)
        energy_ref[lines, :] = energy
        weighed = energy.astype(jnp.float32) * deriv_ref[lines, :].astype(jnp.float32)
        terms = terms + jnp.sum(weighed.reshape(-1, 8, plan.cols_here), axis=0)
    terms = jnp.sum(terms, axis=0, keepdims=True)
    count = FRAG_DEV * plan.cols
    fragment = lax.broadcasted_iota(jnp.int32, (count, BLK), 0)
    sums = jnp.zeros((count, BLK), jnp.float32)
    for j in range(plan.block_cols):
        owner = frag_ref[lax.axis_index("col") * plan.block_cols + j]
        line = jnp.broadcast_to(terms[:, j * BLK : (j + 1) * BLK], (count, BLK))
        sums = sums + jnp.where(fragment == owner, line, 0.0)
    sums_ref[...] = sums


def body(ham, deriv, band, frag_of):
    plan = Plan(*ham.shape)
    bind = functools.partial
    block = jax.ShapeDtypeStruct(ham.shape, jnp.bfloat16)
    total_type = jax.ShapeDtypeStruct(ham.shape, jnp.float32)
    slab_type = jax.ShapeDtypeStruct((plan.rows_here, plan.order), jnp.bfloat16)
    column_type = jax.ShapeDtypeStruct((plan.order, plan.cols_here), jnp.bfloat16)
    others = range(plan.rows)

    def exchange_start(value):
        return [plan.across(value, other) for other in range(2, plan.rows, 2)]

    def exchange_end(first_two, crossed):
        return list(first_two) + [piece for value in crossed for piece in (value, plan.across(value, 1))]

    def gather(mine, partner, hand_over):
        shards = [mine]
        for distance in range(1, plan.far):
            mine = plan.ring(mine)
            last = distance == plan.far - 1 and not hand_over
            partner = plan.ring(partner, last)
            shards += [mine, partner if last else plan.across(partner, 1)]
        return shards, plan.ring(mine)

    partner = plan.across(ham, 1)
    shards, far = gather(ham, partner, False)
    column = exchange_end([ham, partner], exchange_start(ham))
    total, right, slab = call(
        bind(start_kernel, plan, near_places(plan, 0, plan.far)),
        [total_type, column_type, slab_type],
        [band],
        column + shards,
    )
    half_type = jax.ShapeDtypeStruct((plan.rows_here // 2, plan.cols_here), jnp.bfloat16)
    *square, slab = call(
        bind(square_kernel, plan), [half_type, half_type, slab_type], [band], [total, right, slab, far], {3: 2}
    )

    crossed = [exchange_start(part) for part in square]
    partner = [plan.across(part, 1) for part in square]
    keys = [(other, part) for other in (0, 1) for part in (0, 1)]
    (total,) = call(bind(some_kernel, plan, keys), [total_type], [], [slab] + square + partner)
    *second, total = lax.optimization_barrier((*crossed[1], total))
    upper, lower = [[plan.across(value, 1) for value in part] for part in (crossed[0], second)]
    evens, odds = list(others)[2::2], list(others)[3::2]
    keys = [(other, 0) for other in evens + odds]
    (total,) = call(bind(more_kernel, plan, keys), [total_type], [], [slab, total] + crossed[0] + upper)
    keys = [(other, 1) for other in evens]
    (total,) = call(bind(more_kernel, plan, keys), [total_type], [], [slab, total] + second)
    keys = [(other, 1) for other in odds]
    sign, density = call(bind(sign_kernel, plan, keys), [block, block], [band], [slab, total] + lower)
    even, odd = [(other, 0) for other in evens], [(other, 0) for other in odds]

    partner = plan.across(density, 1)
    shards, far = gather(density, partner, True)
    column = exchange_end([density, partner], exchange_start(density))
    (total,) = call(bind(some_kernel, plan, [(0, 0), (1, 0)]), [total_type], [], [slab] + column[:2])
    (total,) = call(bind(more_kernel, plan, even), [total_type], [], [slab, total] + column[2::2])
    (weighted,) = call(bind(weighted_kernel, plan, odd), [block], [band], [slab, total] + column[3::2])
    column = exchange_end([weighted, plan.across(weighted, 1)], exchange_start(weighted))
    (sign_iterate,) = call(copy_kernel, [block], [], [sign])
    shards[0], sign_iterate = lax.optimization_barrier((shards[0], sign_iterate))
    places = near_places(plan, 0, plan.far)
    late = [shards[-1], far]
    total, right = call(bind(near_kernel, plan, places[:-1]), [total_type, column_type], [], column + shards[:-1])
    energy_density, sums = call(
        bind(energy_kernel, plan, places[-1:] + [(plan.far, True)]),
        [block, jax.ShapeDtypeStruct((FRAG_DEV * plan.cols, BLK), jnp.float32)],
        [band, frag_of],
        [total, right, deriv] + late,
    )
    sums = sums.reshape(1, plan.cols, FRAG_DEV, BLK)
    sums = jnp.broadcast_to(sums, (plan.rows, plan.cols, FRAG_DEV, BLK))
    sums = sums.reshape(plan.rows * plan.cols, FRAG_DEV, BLK)
    pulay_terms = jnp.sum(lax.all_to_all(sums, AXES, 0, 0), axis=0)
    return (sign_iterate, energy_density, pulay_terms)


def solution(mesh):
    placed = (P("row", "col"), P("row", "col"), P(), P())
    return jax.shard_map(
        body,
        mesh=mesh,
        in_specs=placed,
        out_specs=(P("row", "col"), P("row", "col"), P("col", None)),
        check_vma=False,
    )
```

```python
import functools

import jax
import jax.numpy as jnp
from jax import lax
from jax.experimental import pallas as pl
from jax.experimental.pallas import tpu as pltpu
from jax.sharding import PartitionSpec as P

BLK = 128
FRAG_DEV = 2
AXES = ("row", "col")
SPAN = 1
SPARE_VMEM = 10 * 1024 * 1024


def cycle_of(count):
    width = 1
    while (2 * width) ** 2 <= count:
        width *= 2
    depth = count // width
    walk = [(step, 0) for step in range(depth)]
    for turn, step in enumerate(range(depth - 1, -1, -1)):
        across = list(range(1, width))
        walk += [(step, place) for place in (across[::-1] if turn % 2 else across)]
    return [step * width + place for step, place in walk]


class Plan:
    def __init__(self, rows_here, cols_here):
        self.rows = lax.axis_size("row")
        self.cols = lax.axis_size("col")
        self.rows_here = rows_here
        self.cols_here = cols_here
        self.order = self.rows * rows_here
        self.block_rows = rows_here // BLK
        self.block_cols = cols_here // BLK
        self.cycle = cycle_of(self.cols)
        self.far = self.cols // 2

    def ring(self, value, to_partner=False):
        pairs = []
        for row in range(self.rows):
            direction = -1 if row % 2 else 1
            target_row = row ^ 1 if to_partner else row
            for place in range(self.cols):
                source = self.cycle[place]
                target = self.cycle[(place + direction) % self.cols]
                pairs.append((row * self.cols + source, target_row * self.cols + target))
        return lax.ppermute(value, AXES, pairs)

    def across(self, value, other):
        return lax.ppermute(value, "row", [(i, i ^ other) for i in range(self.rows)])

    def origin_first(self, distance, behind):
        col = lax.axis_index("col")
        forward = (lax.axis_index("row") % 2 == 0) == behind
        origin = jnp.int32(0)
        for place in range(self.cols):
            before = self.cycle[(place - distance) % self.cols]
            after = self.cycle[(place + distance) % self.cols]
            source = jnp.where(forward, jnp.int32(before), jnp.int32(after))
            origin = jnp.where(col == self.cycle[place], source, origin)
        return pl.multiple_of(origin * self.cols_here, self.cols_here)

    def row_first(self, other):
        return pl.multiple_of((lax.axis_index("row") ^ other) * self.rows_here, self.rows_here)


def spans(plan):
    step = min(SPAN, plan.block_rows)
    return [(i, slice(i * BLK, min(i + step, plan.block_rows) * BLK)) for i in range(0, plan.block_rows, step)]


def masked(plan, band_ref, value, first_block):
    lines = []
    for i in range(value.shape[0] // BLK):
        line = []
        for j in range(plan.block_cols):
            row = lax.axis_index("row") * plan.block_rows + first_block + i
            col = lax.axis_index("col") * plan.block_cols + j
            keep = jnp.abs(row - col) <= jnp.maximum(band_ref[row], band_ref[col])
            block = value[i * BLK : (i + 1) * BLK, j * BLK : (j + 1) * BLK]
            line.append(block * keep.astype(jnp.float32))
        lines.append(jnp.concatenate(line, axis=1))
    return jnp.concatenate(lines, axis=0)


def dot(left, right):
    return jnp.dot(left, right, preferred_element_type=jnp.float32)


def call(kernel, outs, scalars, arrays, aliases=None):
    vmem = pl.BlockSpec(memory_space=pltpu.VMEM)
    smem = pl.BlockSpec(memory_space=pltpu.SMEM)
    moved = sum(a.size * a.dtype.itemsize for a in list(arrays) + list(outs))
    return pl.pallas_call(
        kernel,
        out_shape=outs,
        in_specs=[smem] * len(scalars) + [vmem] * len(arrays),
        out_specs=[vmem] * len(outs),
        input_output_aliases=aliases or {},
        compiler_params=pltpu.CompilerParams(vmem_limit_bytes=moved + SPARE_VMEM),
        cost_estimate=pl.CostEstimate(flops=0, bytes_accessed=0, transcendentals=0),
    )(*scalars, *arrays)


def lay_masked(plan, band_ref, to_ref, from_ref, row_first, col_first, to_row, to_col):
    for i in range(plan.block_rows):
        for j in range(plan.block_cols):
            row, col = row_first // BLK + i, col_first // BLK + j
            keep = jnp.abs(row - col) <= jnp.maximum(band_ref[row], band_ref[col])
            block = from_ref[i * BLK : (i + 1) * BLK, j * BLK : (j + 1) * BLK]
            lines = pl.ds(pl.multiple_of(to_row + i * BLK, BLK), BLK)
            lanes = pl.ds(pl.multiple_of(to_col + j * BLK, BLK), BLK)
            to_ref[lines, lanes] = block * keep.astype(jnp.bfloat16)


def near_places(plan, first, last):
    return [(distance, behind) for distance in range(first, last) for behind in ((True, False) if distance else (True,))]


def start_terms(plan, places, band_ref, right_ref, slab_ref, lefts):
    total = None
    for (distance, behind), left in zip(places, lefts):
        first = plan.origin_first(distance, behind)
        lay_masked(plan, band_ref, slab_ref, left, plan.row_first(0), first, 0, first)
        lanes = pl.ds(first, plan.cols_here)
        term = dot(slab_ref[:, lanes], right_ref[lanes, :])
        total = term if total is None else total + term
    return total


def start_kernel(plan, places, band_ref, *refs):
    rights, refs = refs[: plan.rows], refs[plan.rows :]
    *lefts, total_ref, right_ref, slab_ref = refs
    col_first = plan.origin_first(0, True)
    for other in range(plan.rows):
        row_first = plan.row_first(other)
        lay_masked(plan, band_ref, right_ref, rights[other], row_first, col_first, row_first, 0)
    total_ref[...] = start_terms(plan, places, band_ref, right_ref, slab_ref, lefts)


def square_kernel(plan, band_ref, before_ref, right_ref, _, far_ref, *refs):
    *out_refs, slab_ref = refs
    first = plan.origin_first(plan.far, True)
    lanes = pl.ds(first, plan.cols_here)
    lay_masked(plan, band_ref, slab_ref, far_ref, plan.row_first(0), first, 0, first)
    half = plan.block_rows // 2
    for block in range(plan.block_rows):
        lines = slice(block * BLK, (block + 1) * BLK)
        total = before_ref[lines, :] + dot(slab_ref[lines, lanes], right_ref[lanes, :])
        place = slice(block % half * BLK, (block % half + 1) * BLK)
        out_refs[block // half][place, :] = masked(plan, band_ref, total, block).astype(jnp.bfloat16)


def near_kernel(plan, places, *refs):
    rights, refs = refs[: plan.rows], refs[plan.rows :]
    *lefts, total_ref, right_ref = refs
    for other in range(plan.rows):
        right_ref[pl.ds(plan.row_first(other), plan.rows_here), :] = rights[other][...]
    total = None
    for (distance, behind), left in zip(places, lefts):
        first = plan.origin_first(distance, behind)
        term = dot(left[...], right_ref[pl.ds(first, plan.cols_here), :])
        total = term if total is None else total + term
    total_ref[...] = total


def slab_terms(plan, slab_ref, pieces, lines=slice(None)):
    total = None
    for (other, part), piece in pieces:
        count = piece.shape[0]
        first = pl.multiple_of(plan.row_first(other) + part * count, count)
        term = dot(slab_ref[lines, pl.ds(first, count)], piece[...])
        total = term if total is None else total + term
    return total


def some_kernel(plan, others, slab_ref, *refs):
    *pieces, total_ref = refs
    total_ref[...] = slab_terms(plan, slab_ref, list(zip(others, pieces)))


def more_kernel(plan, others, slab_ref, before_ref, *refs):
    *pieces, total_ref = refs
    total_ref[...] = before_ref[...] + slab_terms(plan, slab_ref, list(zip(others, pieces)))


def sign_kernel(plan, others, band_ref, slab_ref, total_ref, *refs):
    *pieces, sign_ref, density_ref = refs
    first_row = lax.axis_index("row") * plan.rows_here
    first_col = plan.origin_first(0, True)
    for block, lines in spans(plan):
        cubic = total_ref[lines, :] + slab_terms(plan, slab_ref, list(zip(others, pieces)), lines)
        start = slab_ref[lines, pl.ds(first_col, plan.cols_here)].astype(jnp.float32)
        sign = masked(plan, band_ref, 1.5 * start - 0.5 * cubic, block).astype(jnp.bfloat16)
        sign_ref[lines, :] = sign
        rows = first_row + block * BLK + lax.broadcasted_iota(jnp.int32, sign.shape, 0)
        cols = first_col + lax.broadcasted_iota(jnp.int32, sign.shape, 1)
        identity = (rows == cols).astype(jnp.float32)
        density_ref[lines, :] = (0.5 * (identity - sign.astype(jnp.float32))).astype(jnp.bfloat16)


def copy_kernel(from_ref, to_ref):
    to_ref[...] = from_ref[...]


def weighted_kernel(plan, others, band_ref, slab_ref, before_ref, *refs):
    *pieces, out_ref = refs
    for block, lines in spans(plan):
        total = before_ref[lines, :] + slab_terms(plan, slab_ref, list(zip(others, pieces)), lines)
        out_ref[lines, :] = masked(plan, band_ref, total, block).astype(jnp.bfloat16)


def energy_kernel(plan, places, band_ref, frag_ref, total_ref, right_ref, deriv_ref, *refs):
    *lefts, energy_ref, sums_ref = refs
    terms = jnp.zeros((8, plan.cols_here), jnp.float32)
    for block, lines in spans(plan):
        total = total_ref[lines, :]
        for (distance, behind), left in zip(places, lefts):
            first = plan.origin_first(distance, behind)
            total = total + dot(left[lines, :], right_ref[pl.ds(first, plan.cols_here), :])
        energy = masked(plan, band_ref, total, block).astype(jnp.bfloat16)
        energy_ref[lines, :] = energy
        weighed = energy.astype(jnp.float32) * deriv_ref[lines, :].astype(jnp.float32)
        terms = terms + jnp.sum(weighed.reshape(-1, 8, plan.cols_here), axis=0)
    terms = jnp.sum(terms, axis=0, keepdims=True)
    count = FRAG_DEV * plan.cols
    fragment = lax.broadcasted_iota(jnp.int32, (count, BLK), 0)
    sums = jnp.zeros((count, BLK), jnp.float32)
    for j in range(plan.block_cols):
        owner = frag_ref[lax.axis_index("col") * plan.block_cols + j]
        line = jnp.broadcast_to(terms[:, j * BLK : (j + 1) * BLK], (count, BLK))
        sums = sums + jnp.where(fragment == owner, line, 0.0)
    for device in range(plan.rows * plan.cols):
        first = device % plan.cols * FRAG_DEV
        sums_ref[device] = sums[first : first + FRAG_DEV, :]


def body(ham, deriv, band, frag_of):
    plan = Plan(*ham.shape)
    bind = functools.partial
    block = jax.ShapeDtypeStruct(ham.shape, jnp.bfloat16)
    total_type = jax.ShapeDtypeStruct(ham.shape, jnp.float32)
    slab_type = jax.ShapeDtypeStruct((plan.rows_here, plan.order), jnp.bfloat16)
    column_type = jax.ShapeDtypeStruct((plan.order, plan.cols_here), jnp.bfloat16)
    others = range(plan.rows)

    def exchange_start(value):
        return [plan.across(value, other) for other in range(2, plan.rows, 2)]

    def exchange_end(first_two, crossed):
        return list(first_two) + [piece for value in crossed for piece in (value, plan.across(value, 1))]

    def gather(mine, partner, hand_over):
        shards = [mine]
        for distance in range(1, plan.far):
            mine = plan.ring(mine)
            last = distance == plan.far - 1 and not hand_over
            partner = plan.ring(partner, last)
            shards += [mine, partner if last else plan.across(partner, 1)]
        return shards, plan.ring(mine)

    partner = plan.across(ham, 1)
    shards, far = gather(ham, partner, False)
    column = exchange_end([ham, partner], exchange_start(ham))
    total, right, slab = call(
        bind(start_kernel, plan, near_places(plan, 0, plan.far)),
        [total_type, column_type, slab_type],
        [band],
        column + shards,
    )
    half_type = jax.ShapeDtypeStruct((plan.rows_here // 2, plan.cols_here), jnp.bfloat16)
    *square, slab = call(
        bind(square_kernel, plan), [half_type, half_type, slab_type], [band], [total, right, slab, far], {3: 2}
    )

    crossed = [exchange_start(part) for part in square]
    partner = [plan.across(part, 1) for part in square]
    keys = [(other, part) for other in (0, 1) for part in (0, 1)]
    (total,) = call(bind(some_kernel, plan, keys), [total_type], [], [slab] + square + partner)
    *second, total = lax.optimization_barrier((*crossed[1], total))
    upper, lower = [[plan.across(value, 1) for value in part] for part in (crossed[0], second)]
    evens, odds = list(others)[2::2], list(others)[3::2]
    keys = [(other, 0) for other in evens + odds]
    (total,) = call(bind(more_kernel, plan, keys), [total_type], [], [slab, total] + crossed[0] + upper)
    keys = [(other, 1) for other in evens]
    (total,) = call(bind(more_kernel, plan, keys), [total_type], [], [slab, total] + second)
    keys = [(other, 1) for other in odds]
    sign, density = call(bind(sign_kernel, plan, keys), [block, block], [band], [slab, total] + lower)
    even, odd = [(other, 0) for other in evens], [(other, 0) for other in odds]

    partner = plan.across(density, 1)
    shards, far = gather(density, partner, True)
    column = exchange_end([density, partner], exchange_start(density))
    (total,) = call(bind(some_kernel, plan, [(0, 0), (1, 0)]), [total_type], [], [slab] + column[:2])
    (total,) = call(bind(more_kernel, plan, even), [total_type], [], [slab, total] + column[2::2])
    (weighted,) = call(bind(weighted_kernel, plan, odd), [block], [band], [slab, total] + column[3::2])
    column = exchange_end([weighted, plan.across(weighted, 1)], exchange_start(weighted))
    (sign_iterate,) = call(copy_kernel, [block], [], [sign])
    shards[0], sign_iterate = lax.optimization_barrier((shards[0], sign_iterate))
    places = near_places(plan, 0, plan.far)
    late = [shards[-1], far]
    total, right = call(bind(near_kernel, plan, places[:-1]), [total_type, column_type], [], column + shards[:-1])
    energy, sums = call(
        bind(energy_kernel, plan, places[-1:] + [(plan.far, True)]),
        [block, jax.ShapeDtypeStruct((plan.rows * plan.cols, FRAG_DEV, BLK), jnp.float32)],
        [band, frag_of],
        [total, right, deriv] + late,
    )
    (energy_density,) = call(copy_kernel, [block], [], [energy])
    pulay_terms = jnp.sum(lax.all_to_all(sums, AXES, 0, 0), axis=0)
    return (sign_iterate, energy_density, pulay_terms)


def solution(mesh):
    placed = (P("row", "col"), P("row", "col"), P(), P())
    return jax.shard_map(
        body,
        mesh=mesh,
        in_specs=placed,
        out_specs=(P("row", "col"), P("row", "col"), P("col", None)),
        check_vma=False,
    )
```
